128 devices in a mesh: mem: 16 (over y_lo, x, core), strip: 8 (over z, y_hi).
Axes of the slice: x: 4, y: 4 (y_hi: 2, y_lo: 2; y = y_hi * 2 + y_lo), z: 4, core: 2. Of those that a mesh axis runs over, the one named last changes fastest.
Arguments:
- state: float32 [256, 3, 65536], P('mem', None, 'strip'), may hold values from -6 to 6
- courant: float32 [65536], P('strip'), may hold values from 0.5 to 0.95
- angle: float32 [65536], P('strip'), may hold values from -0.4 to 0.4
- obs_index: int32 [4096], P('strip'), may hold values from 0 to 8191
- obs_value: float32 [4096], P('strip'), may hold values from -6 to 6
- obs_variance: float32 [4096], P('strip'), may hold values from 0.1 to 1
- perturb: float32 [256, 4096], P(None, 'strip'), may hold values from -4 to 4
Outputs:
- forecast: float32 [256, 3, 65536], P('mem', None, 'strip')
The draws below stay inside these ranges and needn't reach their ends.
All inputs are finite; a program needn't handle non-finite values.
Results may differ from the reference program's by a relative error of at most 0.00014.
Values sent between devices are 32-bit elements; how exact they have to be, the bound alone decides.
A program may use at most 128 MiB of HBM per device.

```python
import math
import jax
import jax.numpy as jnp
from jax import lax

COLS_DEV = 8192
NOBS = 512
STEPS_BEFORE = 4
STEPS_AFTER = 2
MEMBERS = 256
COLUMNS = 65536
ALL_OBS = 4096


def set_ends(array, own_key, smallest, high):
    place = [jax.random.randint(jax.random.fold_in(own_key, axis), (), 0, length) for axis, length in enumerate(array.shape)]
    widest = array.shape.index(max(array.shape))
    neighbour = place[:widest] + [(place[widest] + 1) % array.shape[widest]] + place[widest + 1:]
    return array.at[tuple(place)].set(smallest).at[tuple(neighbour)].set(high)


def level_of(stream_key, dims, pieces, low, high):
    def one(axis_at, blocks):
        heights = jax.random.uniform(jax.random.fold_in(jax.random.fold_in(stream_key, 6), axis_at), (blocks,), jnp.float32, low / len(pieces), high / len(pieces))
        return jnp.repeat(jnp.exp(heights), dims[axis_at] // blocks).reshape((-1,) + (1,) * (len(dims) - axis_at - 1))

    level = one(*pieces[0])
    for cut in pieces[1:]:
        level = level * one(*cut)
    return level


def gaussian(own_key, shape, width, most, shards=(), kind=jnp.bfloat16):
    values = jax.random.normal(own_key, shape, jnp.float32) * width
    if len(shards) > 0:
        values = level_of(own_key, shape, shards, -0.22, 0.18) * values
    return jnp.clip(values, min=-most, max=most).astype(kind)


def setup_inputs(seed: int = 0) -> dict:
    seeds = jax.random.split(jax.random.key(seed), 8)
    return {
        "state": gaussian(seeds[0], (MEMBERS, 3, COLUMNS), 1.0, 6.0, ((0, 16), (2, 8)), jnp.float32),
        "courant": jnp.clip(0.5 + 0.45 * jax.random.uniform(seeds[1], (COLUMNS,), jnp.float32) ** level_of(seeds[1], (COLUMNS,), ((0, 8),), -0.2, 0.2), 0.5, 0.95),
        "angle": jnp.clip(jax.random.uniform(seeds[2], (COLUMNS,), jnp.float32, -0.4, 0.4) * level_of(seeds[2], (COLUMNS,), ((0, 8),), -0.4, 0.0), -0.4, 0.4),
        "obs_index": set_ends(jax.random.randint(seeds[3], (ALL_OBS,), 0, COLS_DEV), jax.random.fold_in(seeds[3], 1), 0, COLS_DEV - 1).astype(jnp.int32),
        "obs_value": gaussian(seeds[4], (ALL_OBS,), 1.0, 6.0, ((0, 8),), jnp.float32),
        "obs_variance": jnp.clip(jnp.exp(math.log(1.0) - 2.3025851 * jax.random.uniform(seeds[5], (ALL_OBS,), jnp.float32) ** level_of(seeds[5], (ALL_OBS,), ((0, 8),), -0.2, 0.2)), 0.1, 1.0),
        "perturb": gaussian(seeds[6], (MEMBERS, ALL_OBS), 0.5, 4.0, ((1, 8),), jnp.float32),
    }


HIGH = lax.Precision.HIGHEST

def advance(state, courant, angle):
    height = state[:, 0]
    speed = state[:, 1]
    across = state[:, 2]
    right_wave = speed + height
    left_wave = speed - height
    right_new = right_wave - courant * (right_wave - jnp.roll(right_wave, 1, axis=-1))
    left_new = left_wave + courant * (jnp.roll(left_wave, -1, axis=-1) - left_wave)
    speed_new = 0.5 * (right_new + left_new)
    height_new = 0.5 * (right_new - left_new)
    cosine = jnp.cos(angle)
    sine = jnp.sin(angle)
    speed_out = cosine * speed_new + sine * across
    across_out = cosine * across - sine * speed_new
    return jnp.stack([height_new, speed_out, across_out], axis=1)

def gain(predicted, obs_value, perturb, obs_variance):
    count = predicted.shape[0]
    spread = predicted - jnp.mean(predicted, axis=0)
    innovation = obs_value[None, :] + perturb - predicted
    cov = jnp.dot(spread.T, spread, precision=HIGH) / (count - 1) + jnp.diag(obs_variance)
    factor = jnp.linalg.cholesky(cov)
    solved = jax.scipy.linalg.cho_solve((factor, True), innovation.T)
    return jnp.dot(spread, solved, precision=HIGH) / (count - 1)

def reference(state, courant, angle, obs_index, obs_value, obs_variance, perturb):
    for step in range(STEPS_BEFORE):
        state = advance(state, courant, angle)
    count = state.shape[0]
    strips = COLUMNS // COLS_DEV
    offsets = jnp.arange(strips * NOBS, dtype=jnp.int32) // NOBS * COLS_DEV
    columns = obs_index.astype(jnp.int32) + offsets
    predicted = state[:, 0][:, columns]
    predicted = predicted.reshape(count, strips, NOBS).transpose(1, 0, 2)
    pert = perturb.reshape(count, strips, NOBS).transpose(1, 0, 2)
    weights = lax.map(lambda group: gain(*group), (predicted, obs_value.reshape(strips, NOBS), pert, obs_variance.reshape(strips, NOBS)))
    grid = state.reshape(count, 3, strips, COLS_DEV)
    grid = grid + jnp.einsum('skm,kfsc->mfsc', weights, grid, precision=HIGH)
    state = grid.reshape(count, 3, strips * COLS_DEV)
    for step in range(STEPS_AFTER):
        state = advance(state, courant, angle)
    return state
```

```python
import functools

import jax
import jax.numpy as jnp
from jax import lax
from jax.experimental import pallas as pl
from jax.experimental.pallas import tpu as pltpu
from jax.sharding import PartitionSpec as P

STEPS_BEFORE = 4
STEPS_AFTER = 2
SQUARINGS = 14
CHUNK = 1024
TILE = 128
MESH = pl.DeviceIdType.MESH
HIGH = lax.Precision.HIGHEST


def dot(a, b, dims=((1,), (0,))):
    return lax.dot_general(a, b, (dims, ((), ())), precision=HIGH, preferred_element_type=jnp.float32)


def cosine_sine(angle):
    t = angle * angle
    cosine = 1.0 + t * (-1 / 2 + t * (1 / 24 + t * (-1 / 720 + t * (1 / 40320 - t * (1 / 3628800)))))
    sine = angle * (1.0 + t * (-1 / 6 + t * (1 / 120 + t * (-1 / 5040 + t * (1 / 362880)))))
    return cosine, sine


def advance(fields, coefs, steps):
    h, u, v = fields
    c, cosine, sine = coefs
    last = h.shape[-1] - 1
    for _ in range(steps):
        a = u + h
        b = u - h
        a = a - c * (a - pltpu.roll(a, 1, axis=1))
        b = b + c * (pltpu.roll(b, last, axis=1) - b)
        speed = 0.5 * (a + b)
        h = 0.5 * (a - b)
        u = cosine * speed + sine * v
        v = cosine * v - sine * speed
    return h, u, v


def kernel(
    state, courant, angle, obs_index, obs_value, obs_variance, perturb, out,
    padded, coef, prior, observed, mine, grid, mixed, analysed,
    local_sem, halo_send, halo_recv, coef_send, coef_recv, obs_send, obs_recv,
    in_send, in_recv, out_send, out_recv, edge_send, edge_recv,
):
    members, columns = state.shape[1], state.shape[2]
    peers = grid.shape[1] // members
    width = grid.shape[2]
    count = peers * members
    nobs = mine.shape[1]
    me = lax.axis_index("mem")
    strip = lax.axis_index("strip")
    strips = lax.axis_size("strip")
    right = (strip + 1) % strips
    left = (strip + strips - 1) % strips

    barrier = pltpu.get_barrier_semaphore()

    def greet(r, carry):
        pl.semaphore_signal(barrier, inc=1, device_id={"mem": (me + r) % peers}, device_id_type=MESH)
        return carry

    lax.fori_loop(1, peers, greet, 0)
    for other in (left, right):
        pl.semaphore_signal(barrier, inc=1, device_id={"strip": other}, device_id_type=MESH)

    load = pltpu.make_async_copy(state, padded.at[:, :, pl.ds(TILE, columns)], local_sem)
    load.start()

    def coefficients(k, carry):
        at = pl.ds(pl.multiple_of(k * CHUNK, CHUNK), CHUNK)
        to = pl.ds(pl.multiple_of(TILE + k * CHUNK, TILE), CHUNK)
        cosine, sine = cosine_sine(jnp.broadcast_to(angle[:, at], (8, CHUNK)))
        coef[0, :, to] = jnp.broadcast_to(courant[:, at], (8, CHUNK))
        coef[1, :, to] = cosine
        coef[2, :, to] = sine
        return carry

    lax.fori_loop(0, columns // CHUNK, coefficients, 0)
    load.wait()

    first, last = pl.ds(TILE, TILE), pl.ds(columns, TILE)
    before, after = pl.ds(0, TILE), pl.ds(columns + TILE, TILE)

    def halo(buffer, send, recv):
        return [
            pltpu.make_async_remote_copy(
                buffer.at[:, :, source], buffer.at[:, :, target], send.at[n], recv.at[n],
                device_id={"strip": other}, device_id_type=MESH,
            )
            for n, (source, target, other) in enumerate([(last, before, right), (first, after, left)])
        ]

    pl.semaphore_wait(barrier, peers + 1)
    halos = halo(padded, halo_send, halo_recv) + halo(coef, coef_send, coef_recv)
    for copy in halos:
        copy.start()

    def steps_of(source, target, offset, steps, k):
        window = pl.ds(pl.multiple_of(k * CHUNK, TILE), CHUNK + 2 * TILE)
        to = pl.ds(pl.multiple_of(offset + k * CHUNK, TILE), CHUNK)
        factors = [coef[f, :, window] for f in range(3)]
        for half in range(members // 8):
            rows = pl.ds(half * 8, 8)
            fields = advance([source[f, rows, window] for f in range(3)], factors, steps)
            for f in range(3):
                target[f, rows, to] = fields[f][:, TILE : TILE + CHUNK]

    chunks = columns // CHUNK

    def before_steps(k, carry):
        steps_of(padded, prior, 0, STEPS_BEFORE, k)
        return carry

    lax.fori_loop(1, chunks - 1, before_steps, 0)
    for copy in halos:
        copy.wait()
    before_steps(0, 0)
    before_steps(chunks - 1, 0)

    groups = nobs // TILE
    tiles = [jnp.broadcast_to(obs_index[g : g + 1, :] // TILE, (8, TILE)) for g in range(groups)]
    lanes = [jnp.broadcast_to(obs_index[g : g + 1, :] % TILE, (8, TILE)) for g in range(groups)]

    def pick(t, found):
        at = pl.ds(pl.multiple_of(t * TILE, TILE), TILE)
        news = []
        for half in range(members // 8):
            heights = prior[0, pl.ds(half * 8, 8), at]
            for g in range(groups):
                value = jnp.take_along_axis(heights, lanes[g], axis=1)
                news.append(jnp.where(tiles[g] == t, value, found[half * groups + g]))
        return tuple(news)

    zero = jnp.zeros((8, TILE), jnp.float32)
    found = lax.fori_loop(0, columns // TILE, pick, (zero,) * (groups * members // 8))
    own = pl.ds(pl.multiple_of(me * members, members), members)
    for half in range(members // 8):
        for g in range(groups):
            mine[pl.ds(half * 8, 8), pl.ds(g * TILE, TILE)] = found[half * groups + g]
    observed[own, :] = mine[...]

    def obs_copy(r):
        return pltpu.make_async_remote_copy(
            mine, observed.at[own, :], obs_send.at[r], obs_recv.at[r],
            device_id={"mem": (me + r) % peers}, device_id_type=MESH,
        )

    def in_copy(r):
        peer = (me + r) % peers
        return pltpu.make_async_remote_copy(
            prior.at[:, :, pl.ds(pl.multiple_of(peer * width, width), width)], grid.at[:, own, :],
            in_send.at[r], in_recv.at[r], device_id={"mem": peer}, device_id_type=MESH,
        )

    def each(make, action):
        def body(r, carry):
            action(make(r))
            return carry

        lax.fori_loop(1, peers, body, 0)

    each(obs_copy, lambda copy: copy.start())
    each(in_copy, lambda copy: copy.start())
    columns_here = pl.ds(pl.multiple_of(me * width, width), width)
    grid[:, own, :] = prior[:, :, columns_here]
    each(obs_copy, lambda copy: copy.wait())

    predicted = observed[...]
    spread = predicted - jnp.sum(predicted, axis=0, keepdims=True) * (1.0 / count)
    innovation = obs_value[...] + perturb[...] - predicted
    scaled = spread / obs_variance[...]
    rows_id = lax.broadcasted_iota(jnp.int32, (count, count), 0)
    cols_id = lax.broadcasted_iota(jnp.int32, (count, count), 1)
    unit = jnp.where(rows_id == cols_id, 1.0, 0.0).astype(jnp.float32)
    low = float(count - 1)
    inner = dot(scaled, spread, ((1,), (1,))) + low * unit
    update = dot(innovation, scaled, ((1,), (1,)))
    high = jnp.max(jnp.sum(jnp.abs(inner), axis=0, keepdims=True), axis=1, keepdims=True)
    rate = 2.0 / (high + low)
    gap = 2.0 * low / (high + low)
    remainder = unit - rate * inner
    update = rate * update
    for n in range(SQUARINGS):
        both = dot(jnp.concatenate([remainder, update], axis=0), remainder)
        shrink = gap * (2.0 - gap)
        scale = 2.0 / (1.0 + shrink)
        gap = scale * shrink
        remainder = scale * both[:count] + (1.0 - scale) * unit
        update = scale * (update + both[count:])
    update = update + dot(update, remainder)

    each(in_copy, lambda copy: copy.wait())

    def out_copy(f, r):
        peer = (me + r) % peers
        return pltpu.make_async_remote_copy(
            mixed.at[f, pl.ds(pl.multiple_of(peer * members, members), members), :],
            analysed.at[f, :, pl.ds(pl.multiple_of(TILE + me * width, TILE), width)],
            out_send.at[f, r], out_recv.at[f, r], device_id={"mem": peer}, device_id_type=MESH,
        )

    for f in range(3):
        block = grid[f]
        mixed[f] = block + dot(update, block)
        each(functools.partial(out_copy, f), lambda copy: copy.start())
    analysed[:, :, pl.ds(pl.multiple_of(TILE + me * width, TILE), width)] = mixed[:, own, :]
    for f in range(3):
        each(functools.partial(out_copy, f), lambda copy: copy.wait())

    edges = halo(analysed, edge_send, edge_recv)
    for copy in edges:
        copy.start()

    def after_steps(k, carry):
        steps_of(analysed, out, 0, STEPS_AFTER, k)
        return carry

    lax.fori_loop(1, chunks - 1, after_steps, 0)
    for copy in edges:
        copy.wait()
    after_steps(0, 0)
    after_steps(chunks - 1, 0)


def local(state, courant, angle, obs_index, obs_value, obs_variance, perturb):
    members, fields, columns = state.shape
    nobs = obs_index.shape[0]
    peers = lax.axis_size("mem")
    count, width = peers * members, columns // peers
    wide = columns + 2 * TILE
    vmem = pl.BlockSpec(memory_space=pltpu.VMEM)
    f32 = jnp.float32
    dma = pltpu.SemaphoreType.DMA
    result = pl.pallas_call(
        kernel,
        out_shape=jax.ShapeDtypeStruct((fields, members, columns), f32),
        in_specs=[pl.BlockSpec(memory_space=pl.ANY)] + [vmem] * 6,
        out_specs=vmem,
        scratch_shapes=[
            pltpu.VMEM((fields, members, wide), f32),
            pltpu.VMEM((3, 8, wide), f32),
            pltpu.VMEM((fields, members, columns), f32),
            pltpu.VMEM((count, nobs), f32),
            pltpu.VMEM((members, nobs), f32),
            pltpu.VMEM((fields, count, width), f32),
            pltpu.VMEM((fields, count, width), f32),
            pltpu.VMEM((fields, members, wide), f32),
            dma,
            dma((2,)), dma((2,)), dma((2,)), dma((2,)),
            dma((peers,)), dma((peers,)), dma((peers,)), dma((peers,)),
            dma((fields, peers)), dma((fields, peers)), dma((2,)), dma((2,)),
        ],
        compiler_params=pltpu.CompilerParams(collective_id=0, has_side_effects=True, vmem_limit_bytes=48 * 2**20),
    )(
        jnp.transpose(state, (1, 0, 2)), courant[None, :], angle[None, :],
        obs_index.reshape(nobs // TILE, TILE), obs_value[None, :], obs_variance[None, :], perturb,
    )
    return jnp.transpose(result, (1, 0, 2))


def solution(mesh):
    in_specs = (
        P("mem", None, "strip"),
        P("strip"),
        P("strip"),
        P("strip"),
        P("strip"),
        P("strip"),
        P(None, "strip"),
    )
    out_specs = P("mem", None, "strip")
    return jax.shard_map(local, mesh=mesh, in_specs=in_specs, out_specs=out_specs, check_vma=False)
```

```python
import functools

import jax
import jax.numpy as jnp
from jax import lax
from jax.experimental import pallas as pl
from jax.experimental.pallas import tpu as pltpu
from jax.sharding import PartitionSpec as P

STEPS_BEFORE = 4
STEPS_AFTER = 2
SQUARINGS = 12
EXACT = 5
CHUNK = 1024
TILE = 128
PICKS = 31
MESH = pl.DeviceIdType.MESH
HIGH = lax.Precision.HIGHEST


def dot(a, b, dims=((1,), (0,))):
    return lax.dot_general(a, b, (dims, ((), ())), precision=HIGH, preferred_element_type=jnp.float32)


def dot3(a, b):
    a_hi, b_hi = a.astype(jnp.bfloat16), b.astype(jnp.bfloat16)
    a_lo = (a - a_hi.astype(jnp.float32)).astype(jnp.bfloat16)
    b_lo = (b - b_hi.astype(jnp.float32)).astype(jnp.bfloat16)
    rows = a.shape[0]
    both = jnp.dot(jnp.concatenate([a_hi, a_lo], axis=0), b_hi, preferred_element_type=jnp.float32)
    return both[:rows] + (both[rows:] + jnp.dot(a_hi, b_lo, preferred_element_type=jnp.float32))


def cosine_sine(angle):
    t = angle * angle
    cosine = 1.0 + t * (-1 / 2 + t * (1 / 24 + t * (-1 / 720 + t * (1 / 40320 - t * (1 / 3628800)))))
    sine = angle * (1.0 + t * (-1 / 6 + t * (1 / 120 + t * (-1 / 5040 + t * (1 / 362880)))))
    return cosine, sine


def advance(fields, coefs, steps):
    h, u, v = fields
    c, cosine, sine = coefs
    last = h.shape[-1] - 1
    for _ in range(steps):
        a = u + h
        b = u - h
        a = a - c * (a - pltpu.roll(a, 1, axis=1))
        b = b + c * (pltpu.roll(b, last, axis=1) - b)
        speed = 0.5 * (a + b)
        h = 0.5 * (a - b)
        u = cosine * speed + sine * v
        v = cosine * v - sine * speed
    return h, u, v


def kernel(
    state, courant, angle, obs_index, obs_value, obs_variance, perturb, out,
    fields_in, raw, coef, index, value, variance, noise, prior, observed, grid, mixed, analysed,
    halo_in, halo_raw, halo_out,
    load_sem, state_sem, halo_send, halo_recv, obs_send, obs_recv,
    in_send, in_recv, out_send, out_recv, edge_send, edge_recv,
):
    members, columns = state.shape[1], state.shape[2]
    peers = grid.shape[1] // members
    width = grid.shape[2]
    parts = width // TILE
    count = peers * members
    nobs = observed.shape[1]
    chunks = columns // CHUNK
    halves = members // 8
    me = lax.axis_index("mem")
    strip = lax.axis_index("strip")
    strips = lax.axis_size("strip")
    right = (strip + 1) % strips
    left = (strip + strips - 1) % strips
    first, last = pl.ds(0, TILE), pl.ds(columns - TILE, TILE)
    own = pl.ds(pl.multiple_of(me * members, members), members)

    barrier = pltpu.get_barrier_semaphore()

    def greet(r, carry):
        pl.semaphore_signal(barrier, inc=1, device_id={"mem": (me + r) % peers}, device_id_type=MESH)
        return carry

    lax.fori_loop(1, peers, greet, 0)
    for other in (left, right):
        pl.semaphore_signal(barrier, inc=1, device_id={"strip": other}, device_id_type=MESH)

    pairs = [
        (angle, raw.at[0]), (courant, raw.at[1]), (obs_index, index), (obs_value, value),
        (obs_variance, variance), (perturb, noise),
    ]
    loads = [pltpu.make_async_copy(a, b, load_sem.at[n]) for n, (a, b) in enumerate(pairs)]

    def state_load(k):
        at = pl.ds(k * CHUNK, CHUNK)
        return pltpu.make_async_copy(state.at[:, :, at], fields_in.at[:, :, at], state_sem.at[k])

    for load in loads[:2]:
        load.start()
    for k in range(chunks):
        state_load(k).start()
    for load in loads[2:]:
        load.start()

    pl.semaphore_wait(barrier, peers + 1)

    def to_neighbours(source, target, send, recv):
        return [
            pltpu.make_async_remote_copy(
                source.at[..., at], target.at[side], send.at[side], recv.at[side],
                device_id={"strip": other}, device_id_type=MESH,
            )
            for side, (at, other) in enumerate([(last, right), (first, left)])
        ]

    halos = (
        to_neighbours(state, halo_in, halo_send.at[0], halo_recv.at[0])
        + to_neighbours(angle, halo_raw.at[0], halo_send.at[1], halo_recv.at[1])
        + to_neighbours(courant, halo_raw.at[1], halo_send.at[2], halo_recv.at[2])
    )
    for copy in halos:
        copy.start()

    for load in loads[:2]:
        load.wait()

    def factors_of(turn, speed):
        shape = (8, turn.shape[-1])
        cosine, sine = cosine_sine(jnp.broadcast_to(turn, shape))
        return jnp.broadcast_to(speed, shape), cosine, sine

    def coefficients(k, carry):
        at = pl.ds(pl.multiple_of(k * CHUNK, CHUNK), CHUNK)
        for f, factor in enumerate(factors_of(raw[0, :, at], raw[1, :, at])):
            coef[f, :, at] = factor
        return carry

    lax.fori_loop(0, chunks, coefficients, 0)

    def sweep(source, target, steps, k, before=TILE, after=TILE):
        window = pl.ds(pl.multiple_of(k * CHUNK - before, TILE), CHUNK + before + after)
        to = pl.ds(pl.multiple_of(k * CHUNK, CHUNK), CHUNK)
        factors = [coef[f, :, window] for f in range(3)]
        for half in range(halves):
            rows = pl.ds(half * 8, 8)
            news = advance([source[f, rows, window] for f in range(3)], factors, steps)
            for f in range(3):
                target[f, rows, to] = news[f][:, before : before + CHUNK]

    def sweep_all(source, target, steps, ready):
        ready(0)
        ready(1)
        sweep(source, target, steps, 0, before=0)

        def body(k, carry):
            ready(k + 1)
            sweep(source, target, steps, k)
            return carry

        lax.fori_loop(1, chunks - 1, body, 0)
        sweep(source, target, steps, chunks - 1, after=0)

    def sweep_ends(source, halo, target, steps, outer):
        two = [pl.ds(columns - 2 * TILE, 2 * TILE), pl.ds(0, 2 * TILE)]
        for side in range(2):
            inner = two[1 - side]

            def joined(edge, inside, side=side):
                return jnp.concatenate([edge, inside] if side == 0 else [inside, edge], axis=1)

            factors = [joined(outer[side][f], coef[f, :, inner]) for f in range(3)]
            for half in range(halves):
                rows = pl.ds(half * 8, 8)
                window = [joined(halo[side, f, rows, :], source[f, rows, inner]) for f in range(3)]
                news = advance(window, factors, steps)
                for f in range(3):
                    target[f, rows, (first, last)[side]] = news[f][:, TILE : 2 * TILE]

    def state_ready(k):
        at = pl.ds(pl.multiple_of(k * CHUNK, CHUNK), CHUNK)
        pltpu.make_async_copy(state.at[:, :, at], fields_in.at[:, :, at], state_sem.at[k]).wait()

    sweep_all(fields_in, prior, STEPS_BEFORE, state_ready)

    def part_of(peer, q):
        return q + (peer // (peers - 1)) * (parts - 1 - 2 * q)

    def in_copy(q, r):
        peer = (me + r) % peers
        t = part_of(peer, q)
        return pltpu.make_async_remote_copy(
            prior.at[:, :, pl.ds(pl.multiple_of(peer * width + t * TILE, TILE), TILE)],
            grid.at[:, own, pl.ds(pl.multiple_of(t * TILE, TILE), TILE)],
            in_send.at[q, r], in_recv.at[q, r], device_id={"mem": peer}, device_id_type=MESH,
        )

    def each(make, action):
        def body(r, carry):
            action(make(r))
            return carry

        lax.fori_loop(1, peers, body, 0)

    each(functools.partial(in_copy, 1), lambda copy: copy.start())

    for load in loads[2:]:
        load.wait()
    groups = nobs // TILE
    tiles = [jnp.broadcast_to(index[g : g + 1, :] // TILE, (8, TILE)) for g in range(groups)]
    lanes = [jnp.broadcast_to(index[g : g + 1, :] % TILE, (8, TILE)) for g in range(groups)]

    def pick(t, found):
        at = pl.ds(pl.multiple_of(t * TILE, TILE), TILE)
        news = []
        for half in range(halves):
            heights = prior[0, pl.ds(half * 8, 8), at]
            for g in range(groups):
                picked = jnp.take_along_axis(heights, lanes[g], axis=1)
                news.append(jnp.where(tiles[g] == t, picked, found[half * groups + g]))
        return tuple(news)

    inside = columns // TILE - 2

    def pick_some(k, found):
        for j in range(PICKS):
            found = pick(1 + k * PICKS + j, found)
        return found

    found = (jnp.zeros((8, TILE), jnp.float32),) * (groups * halves)
    found = lax.fori_loop(0, inside // PICKS, pick_some, found)

    for copy in halos:
        copy.wait()
    outer = [factors_of(halo_raw[0, side], halo_raw[1, side]) for side in range(2)]
    sweep_ends(fields_in, halo_in, prior, STEPS_BEFORE, outer)
    found = pick(0, found)
    found = pick(columns // TILE - 1, found)
    for half in range(halves):
        for g in range(groups):
            rows = pl.ds(pl.multiple_of(me * members + half * 8, 8), 8)
            observed[rows, pl.ds(g * TILE, TILE)] = found[half * groups + g]

    def obs_copy(r):
        return pltpu.make_async_remote_copy(
            observed.at[own, :], observed.at[own, :], obs_send.at[r], obs_recv.at[r],
            device_id={"mem": (me + r) % peers}, device_id_type=MESH,
        )

    each(obs_copy, lambda copy: copy.start())
    for q in (0, 2, 3):
        each(functools.partial(in_copy, q), lambda copy: copy.start())
    grid[:, own, :] = prior[:, :, pl.ds(pl.multiple_of(me * width, width), width)]
    each(obs_copy, lambda copy: copy.wait())

    predicted = observed[...]
    spread = predicted - jnp.sum(predicted, axis=0, keepdims=True) * (1.0 / count)
    innovation = value[...] + noise[...] - predicted
    scaled = spread / variance[...]
    rows_id = lax.broadcasted_iota(jnp.int32, (count, count), 0)
    cols_id = lax.broadcasted_iota(jnp.int32, (count, count), 1)
    unit = jnp.where(rows_id == cols_id, 1.0, 0.0).astype(jnp.float32)
    low = float(count - 1)
    inner = dot(scaled, spread, ((1,), (1,))) + low * unit
    update = dot(innovation, scaled, ((1,), (1,)))
    widest = jnp.max(jnp.sum(jnp.abs(inner), axis=0, keepdims=True), axis=1, keepdims=True)
    total = jnp.sum(jnp.sum(inner * unit, axis=0, keepdims=True), axis=1, keepdims=True)
    high = jnp.minimum(widest, total)
    rate = 2.0 / (high + low)
    gap = 2.0 * low / (high + low)
    remainder = unit - rate * inner
    inverse = rate * unit
    for n in range(SQUARINGS):
        multiply = dot if n < EXACT else dot3
        shrink = gap * (2.0 - gap)
        scale = 2.0 / (1.0 + shrink)
        gap = scale * shrink
        if n == 0:
            inverse = (scale * rate) * (unit + remainder)
            square = multiply(remainder, remainder)
        else:
            both = multiply(jnp.concatenate([remainder, inverse], axis=0), remainder)
            square, inverse = both[:count], scale * (inverse + both[count:])
        remainder = scale * square + (1.0 - scale) * unit
    inverse = inverse + dot3(inverse, remainder)
    first_try = dot3(update, inverse)
    update = first_try + dot3(update - dot(first_try, inner), inverse)

    def out_copy(q, r):
        peer = (me + r) % peers
        t = part_of(me, q)
        return pltpu.make_async_remote_copy(
            mixed.at[:, pl.ds(pl.multiple_of(peer * members, members), members), pl.ds(pl.multiple_of(t * TILE, TILE), TILE)],
            analysed.at[:, :, pl.ds(pl.multiple_of(me * width + t * TILE, TILE), TILE)],
            out_send.at[q, r], out_recv.at[q, r], device_id={"mem": peer}, device_id_type=MESH,
        )

    for q in range(parts):
        each(functools.partial(in_copy, q), lambda copy: copy.wait())
        at = pl.ds(pl.multiple_of(part_of(me, q) * TILE, TILE), TILE)
        block = jnp.concatenate([grid[f, :, at] for f in range(3)], axis=1)
        block = block + dot3(update, block)
        for f in range(3):
            mixed[f, :, at] = block[:, f * TILE : (f + 1) * TILE]
        each(functools.partial(out_copy, q), lambda copy: copy.start())
    analysed[:, :, pl.ds(pl.multiple_of(me * width, width), width)] = mixed[:, own, :]
    each(functools.partial(out_copy, 0), lambda copy: copy.wait())
    edges = to_neighbours(analysed, halo_out, edge_send, edge_recv)
    for copy in edges:
        copy.start()
    for q in range(1, parts):
        each(functools.partial(out_copy, q), lambda copy: copy.wait())
    sweep_all(analysed, out, STEPS_AFTER, lambda k: None)
    for copy in edges:
        copy.wait()
    sweep_ends(analysed, halo_out, out, STEPS_AFTER, outer)


def local(state, courant, angle, obs_index, obs_value, obs_variance, perturb):
    members, fields, columns = state.shape
    nobs = obs_index.shape[0]
    peers = lax.axis_size("mem")
    count, width = peers * members, columns // peers
    parts = width // TILE
    f32 = jnp.float32
    dma = pltpu.SemaphoreType.DMA
    result = pl.pallas_call(
        kernel,
        out_shape=pltpu.VMEM((fields, members, columns), f32),
        in_specs=[pl.BlockSpec(memory_space=pltpu.HBM)] * 7,
        out_specs=pl.BlockSpec(memory_space=pltpu.VMEM),
        scratch_shapes=[
            pltpu.VMEM((fields, members, columns), f32),
            pltpu.VMEM((2, 1, columns), f32),
            pltpu.VMEM((3, 8, columns), f32),
            pltpu.VMEM((nobs // TILE, TILE), jnp.int32),
            pltpu.VMEM((1, nobs), f32),
            pltpu.VMEM((1, nobs), f32),
            pltpu.VMEM((count, nobs), f32),
            pltpu.VMEM((fields, members, columns), f32),
            pltpu.VMEM((count, nobs), f32),
            pltpu.VMEM((fields, count, width), f32),
            pltpu.VMEM((fields, count, width), f32),
            pltpu.VMEM((fields, members, columns), f32),
            pltpu.VMEM((2, fields, members, TILE), f32),
            pltpu.VMEM((2, 2, 1, TILE), f32),
            pltpu.VMEM((2, fields, members, TILE), f32),
            dma((6,)), dma((columns // CHUNK,)), dma((3, 2)), dma((3, 2)), dma((peers,)), dma((peers,)),
            dma((parts, peers)), dma((parts, peers)), dma((parts, peers)), dma((parts, peers)), dma((2,)), dma((2,)),
        ],
        compiler_params=pltpu.CompilerParams(collective_id=0, has_side_effects=True, vmem_limit_bytes=60 * 2**20),
    )(
        jnp.transpose(state, (1, 0, 2)), courant[None, :], angle[None, :],
        obs_index.reshape(nobs // TILE, TILE), obs_value[None, :], obs_variance[None, :], perturb,
    )
    return jnp.transpose(result, (1, 0, 2))


def solution(mesh):
    in_specs = (
        P("mem", None, "strip"),
        P("strip"),
        P("strip"),
        P("strip"),
        P("strip"),
        P("strip"),
        P(None, "strip"),
    )
    out_specs = P("mem", None, "strip")
    return jax.shard_map(local, mesh=mesh, in_specs=in_specs, out_specs=out_specs, check_vma=False)
```

```python
import functools

import jax
import jax.numpy as jnp
from jax import lax
from jax.experimental import pallas as pl
from jax.experimental.pallas import tpu as pltpu
from jax.sharding import PartitionSpec as P

STEPS_BEFORE = 4
STEPS_AFTER = 2
SQUARINGS = 12
EXACT = 4
ROUGH = 2
CHUNK = 1024
TILE = 128
MESH = pl.DeviceIdType.MESH
HIGH = lax.Precision.HIGHEST


def dot(a, b, dims=((1,), (0,))):
    return lax.dot_general(a, b, (dims, ((), ())), precision=HIGH, preferred_element_type=jnp.float32)


def dot3(a, b, dims=((1,), (0,))):
    def one(x, y):
        return lax.dot_general(x, y, (dims, ((), ())), preferred_element_type=jnp.float32)

    a_hi, b_hi = a.astype(jnp.bfloat16), b.astype(jnp.bfloat16)
    a_lo = (a - a_hi.astype(jnp.float32)).astype(jnp.bfloat16)
    b_lo = (b - b_hi.astype(jnp.float32)).astype(jnp.bfloat16)
    rows = a.shape[0]
    both = one(jnp.concatenate([a_hi, a_lo], axis=0), b_hi)
    return both[:rows] + (both[rows:] + one(a_hi, b_lo))


def dot1(a, b):
    return jnp.dot(a.astype(jnp.bfloat16), b.astype(jnp.bfloat16), preferred_element_type=jnp.float32)


def cosine_sine(angle):
    t = angle * angle
    cosine = 1.0 + t * (-1 / 2 + t * (1 / 24 + t * (-1 / 720 + t * (1 / 40320 - t * (1 / 3628800)))))
    sine = angle * (1.0 + t * (-1 / 6 + t * (1 / 120 + t * (-1 / 5040 + t * (1 / 362880)))))
    return cosine, sine


def advance(fields, coefs, steps):
    h, u, v = fields
    c, cosine, sine = coefs
    last = h.shape[-1] - 1
    for _ in range(steps):
        a = u + h
        b = u - h
        a = a - c * (a - pltpu.roll(a, 1, axis=1))
        b = b + c * (pltpu.roll(b, last, axis=1) - b)
        speed = 0.5 * (a + b)
        h = 0.5 * (a - b)
        u = cosine * speed + sine * v
        v = cosine * v - sine * speed
    return h, u, v


def kernel(
    state, courant, angle, obs_index, obs_value, obs_variance, perturb, out,
    fields_in, raw, coef, index, value, variance, noise, prior, observed, grid, mixed, analysed,
    halo_in, halo_raw, halo_out,
    load_sem, state_sem, halo_send, halo_recv, obs_send, obs_recv,
    in_send, in_recv, out_send, out_recv, edge_send, edge_recv,
):
    members, columns = state.shape[1], state.shape[2]
    peers = grid.shape[1] // members
    width = grid.shape[2]
    parts = width // TILE
    count = peers * members
    nobs = observed.shape[1]
    chunks = columns // CHUNK
    halves = members // 8
    me = lax.axis_index("mem")
    strip = lax.axis_index("strip")
    strips = lax.axis_size("strip")
    right = (strip + 1) % strips
    left = (strip + strips - 1) % strips
    first, last = pl.ds(0, TILE), pl.ds(columns - TILE, TILE)
    own = pl.ds(pl.multiple_of(me * members, members), members)

    barrier = pltpu.get_barrier_semaphore()

    def greet(r, carry):
        pl.semaphore_signal(barrier, inc=1, device_id={"mem": (me + r) % peers}, device_id_type=MESH)
        return carry

    lax.fori_loop(1, peers, greet, 0)
    for other in (left, right):
        pl.semaphore_signal(barrier, inc=1, device_id={"strip": other}, device_id_type=MESH)

    pairs = [
        (angle, raw.at[0]), (courant, raw.at[1]), (obs_index, index), (obs_value, value),
        (obs_variance, variance), (perturb, noise),
    ]
    loads = [pltpu.make_async_copy(a, b, load_sem.at[n]) for n, (a, b) in enumerate(pairs)]

    def state_load(k):
        at = pl.ds(k * CHUNK, CHUNK)
        to = pl.ds(TILE + k * CHUNK, CHUNK)
        return pltpu.make_async_copy(state.at[:, :, at], fields_in.at[:, :, to], state_sem.at[k])

    for load in loads[:2]:
        load.start()
    for k in range(chunks):
        state_load(k).start()
    for load in loads[2:]:
        load.start()

    pl.semaphore_wait(barrier, peers + 1)

    def to_neighbours(source, target, send, recv):
        return [
            pltpu.make_async_remote_copy(
                source.at[..., at], target.at[side], send.at[side], recv.at[side],
                device_id={"strip": other}, device_id_type=MESH,
            )
            for side, (at, other) in enumerate([(last, right), (first, left)])
        ]

    halos = (
        to_neighbours(state, halo_in, halo_send.at[0], halo_recv.at[0])
        + to_neighbours(angle, halo_raw.at[0], halo_send.at[1], halo_recv.at[1])
        + to_neighbours(courant, halo_raw.at[1], halo_send.at[2], halo_recv.at[2])
    )
    for copy in halos:
        copy.start()

    for load in loads[:2]:
        load.wait()

    def factors_of(turn, speed):
        shape = (8, turn.shape[-1])
        cosine, sine = cosine_sine(jnp.broadcast_to(turn, shape))
        return jnp.broadcast_to(speed, shape), cosine, sine

    def coefficients(k, carry):
        at = pl.ds(pl.multiple_of(k * CHUNK, CHUNK), CHUNK)
        to = pl.ds(pl.multiple_of(TILE + k * CHUNK, TILE), CHUNK)
        for f, factor in enumerate(factors_of(raw[0, :, at], raw[1, :, at])):
            coef[f, :, to] = factor
        return carry

    lax.fori_loop(0, chunks, coefficients, 0)

    def sweep(source, target, steps, k):
        window = pl.ds(pl.multiple_of(k * CHUNK, TILE), CHUNK + 2 * TILE)
        to = pl.ds(pl.multiple_of(k * CHUNK, CHUNK), CHUNK)
        factors = [coef[f, :, window] for f in range(3)]
        for half in range(halves):
            rows = pl.ds(half * 8, 8)
            news = advance([source[f, rows, window] for f in range(3)], factors, steps)
            for f in range(3):
                target[f, rows, to] = news[f][:, TILE : TILE + CHUNK]

    def sweep_ends(source, halo, target, steps, outer):
        two = [pl.ds(columns - TILE, 2 * TILE), pl.ds(TILE, 2 * TILE)]
        for side in range(2):
            inner = two[1 - side]

            def joined(edge, inside, side=side):
                return jnp.concatenate([edge, inside] if side == 0 else [inside, edge], axis=1)

            factors = [joined(outer[side][f], coef[f, :, inner]) for f in range(3)]
            for half in range(halves):
                rows = pl.ds(half * 8, 8)
                window = [joined(halo[side, f, rows, :], source[f, rows, inner]) for f in range(3)]
                news = advance(window, factors, steps)
                for f in range(3):
                    target[f, rows, (first, last)[side]] = news[f][:, TILE : 2 * TILE]

    for k in range(chunks):
        state_load(k).wait()

    def part_of(peer, q):
        return q + (peer // (peers - 1)) * (parts - 1 - 2 * q)

    def in_copy(q, r):
        peer = (me + r) % peers
        t = part_of(peer, q)
        return pltpu.make_async_remote_copy(
            prior.at[:, :, pl.ds(pl.multiple_of(peer * width + t * TILE, TILE), TILE)],
            grid.at[:, own, pl.ds(pl.multiple_of(t * TILE, TILE), TILE)],
            in_send.at[q, r], in_recv.at[q, r], device_id={"mem": peer}, device_id_type=MESH,
        )

    def each(make, action):
        def body(r, carry):
            action(make(r))
            return carry

        lax.fori_loop(1, peers, body, 0)

    for load in loads[2:]:
        load.wait()
    groups = nobs // TILE
    tiles = [jnp.broadcast_to(index[g : g + 1, :] // TILE, (8, TILE)) for g in range(groups)]
    lanes = [jnp.broadcast_to(index[g : g + 1, :] % TILE, (8, TILE)) for g in range(groups)]

    def pick(t, found):
        at = pl.ds(pl.multiple_of(t * TILE, TILE), TILE)
        news = []
        for half in range(halves):
            heights = prior[0, pl.ds(half * 8, 8), at]
            for g in range(groups):
                picked = jnp.take_along_axis(heights, lanes[g], axis=1)
                news.append(jnp.where(tiles[g] == t, picked, found[half * groups + g]))
        return tuple(news)

    blocks = CHUNK // width

    def step_and_send(i, found):
        k = (me // blocks + 1 + i) % chunks
        sweep(fields_in, prior, STEPS_BEFORE, k)
        for j in range(CHUNK // TILE):
            found = pick(k * (CHUNK // TILE) + j, found)
        for j in range(blocks):
            peer = k * blocks + j

            @pl.when(peer != me)
            def _(peer=peer):
                in_copy(1, (peer + peers - me) % peers).start()

        return found

    found = (jnp.zeros((8, TILE), jnp.float32),) * (groups * halves)
    found = lax.fori_loop(0, chunks, step_and_send, found)

    for copy in halos:
        copy.wait()
    outer = [factors_of(halo_raw[0, side], halo_raw[1, side]) for side in range(2)]
    sweep_ends(fields_in, halo_in, prior, STEPS_BEFORE, outer)
    found = pick(0, found)
    found = pick(columns // TILE - 1, found)
    for half in range(halves):
        for g in range(groups):
            rows = pl.ds(pl.multiple_of(me * members + half * 8, 8), 8)
            observed[rows, pl.ds(g * TILE, TILE)] = found[half * groups + g]

    chips = peers // 2
    sibling = me + 1 - 2 * (me % 2)

    def obs_copy(r):
        return pltpu.make_async_remote_copy(
            observed.at[own, :], observed.at[own, :], obs_send.at[r], obs_recv.at[r],
            device_id={"mem": (me + 2 * r) % peers}, device_id_type=MESH,
        )

    def obs_share(r):
        rows = pl.ds(pl.multiple_of((me + peers - 2 * r) % peers * members, members), members)
        return pltpu.make_async_remote_copy(
            observed.at[rows, :], observed.at[rows, :], obs_send.at[chips + r], obs_recv.at[chips + r],
            device_id={"mem": sibling}, device_id_type=MESH,
        )

    for r in range(1, chips):
        obs_copy(r).start()
    obs_share(0).start()
    for q in (0, 2, 3):
        each(functools.partial(in_copy, q), lambda copy: copy.start())
    grid[:, own, :] = prior[:, :, pl.ds(pl.multiple_of(me * width, width), width)]
    for r in range(1, chips):
        obs_copy(r).wait_recv()
        obs_share(r).start()
    for r in range(chips):
        obs_share(r).wait()
    for r in range(1, chips):
        obs_copy(r).wait_send()

    predicted = observed[...]
    spread = predicted - jnp.sum(predicted, axis=0, keepdims=True) * (1.0 / count)
    innovation = value[...] + noise[...] - predicted
    scaled = spread * (1.0 / variance[...])
    rows_id = lax.broadcasted_iota(jnp.int32, (count, count), 0)
    cols_id = lax.broadcasted_iota(jnp.int32, (count, count), 1)
    unit = jnp.where(rows_id == cols_id, 1.0, 0.0).astype(jnp.float32)
    low = float(count - 1)
    inner = dot(scaled, spread, ((1,), (1,))) + low * unit
    update = dot(innovation, scaled, ((1,), (1,)))
    widest = jnp.max(jnp.sum(jnp.abs(inner), axis=0, keepdims=True), axis=1, keepdims=True)
    total = jnp.sum(jnp.sum(inner * unit, axis=0, keepdims=True), axis=1, keepdims=True)
    high = jnp.minimum(widest, total)
    rate = 2.0 / (high + low)
    gap = 2.0 * low / (high + low)
    remainder = unit - rate * inner
    inverse = rate * unit
    for n in range(SQUARINGS):
        multiply = dot if n < EXACT else dot3 if n < SQUARINGS - ROUGH else dot1
        shrink = gap * (2.0 - gap)
        scale = 2.0 / (1.0 + shrink)
        gap = scale * shrink
        if n == 0:
            inverse = (scale * rate) * (unit + remainder)
            square = multiply(remainder, remainder)
        else:
            both = multiply(jnp.concatenate([remainder, inverse], axis=0), remainder)
            square, inverse = both[:count], scale * (inverse + both[count:])
        remainder = scale * square + (1.0 - scale) * unit
    inverse = inverse + dot1(inverse, remainder)
    first_try = dot(update, inverse)
    update = first_try + dot3(update - dot(first_try, inner), inverse)

    def out_copy(q, r):
        peer = (me + r) % peers
        t = part_of(me, q)
        return pltpu.make_async_remote_copy(
            mixed.at[:, pl.ds(pl.multiple_of(peer * members, members), members), pl.ds(pl.multiple_of(t * TILE, TILE), TILE)],
            analysed.at[:, :, pl.ds(pl.multiple_of(TILE + me * width + t * TILE, TILE), TILE)],
            out_send.at[q, r], out_recv.at[q, r], device_id={"mem": peer}, device_id_type=MESH,
        )

    for q in range(parts):
        each(functools.partial(in_copy, q), lambda copy: copy.wait())
        at = pl.ds(pl.multiple_of(part_of(me, q) * TILE, TILE), TILE)
        block = jnp.concatenate([grid[f, :, at] for f in range(3)], axis=1)
        block = block + dot3(update, block)
        for f in range(3):
            mixed[f, :, at] = block[:, f * TILE : (f + 1) * TILE]
        each(functools.partial(out_copy, q), lambda copy: copy.start())
    analysed[:, :, pl.ds(pl.multiple_of(TILE + me * width, TILE), width)] = mixed[:, own, :]
    each(functools.partial(out_copy, 0), lambda copy: copy.wait())
    edges = to_neighbours(analysed.at[:, :, pl.ds(TILE, columns)], halo_out, edge_send, edge_recv)
    for copy in edges:
        copy.start()
    for q in range(1, parts):
        each(functools.partial(out_copy, q), lambda copy: copy.wait())

    def last_steps(k, carry):
        sweep(analysed, out, STEPS_AFTER, k)
        return carry

    lax.fori_loop(0, chunks, last_steps, 0)
    for copy in edges:
        copy.wait()
    sweep_ends(analysed, halo_out, out, STEPS_AFTER, outer)


def local(state, courant, angle, obs_index, obs_value, obs_variance, perturb):
    members, fields, columns = state.shape
    nobs = obs_index.shape[0]
    peers = lax.axis_size("mem")
    count, width = peers * members, columns // peers
    parts, wide = width // TILE, columns + 2 * TILE
    f32 = jnp.float32
    dma = pltpu.SemaphoreType.DMA
    result = pl.pallas_call(
        kernel,
        out_shape=pltpu.VMEM((fields, members, columns), f32),
        in_specs=[pl.BlockSpec(memory_space=pltpu.HBM)] * 7,
        out_specs=pl.BlockSpec(memory_space=pltpu.VMEM),
        scratch_shapes=[
            pltpu.VMEM((fields, members, wide), f32),
            pltpu.VMEM((2, 1, columns), f32),
            pltpu.VMEM((3, 8, wide), f32),
            pltpu.VMEM((nobs // TILE, TILE), jnp.int32),
            pltpu.VMEM((1, nobs), f32),
            pltpu.VMEM((1, nobs), f32),
            pltpu.VMEM((count, nobs), f32),
            pltpu.VMEM((fields, members, columns), f32),
            pltpu.VMEM((count, nobs), f32),
            pltpu.VMEM((fields, count, width), f32),
            pltpu.VMEM((fields, count, width), f32),
            pltpu.VMEM((fields, members, wide), f32),
            pltpu.VMEM((2, fields, members, TILE), f32),
            pltpu.VMEM((2, 2, 1, TILE), f32),
            pltpu.VMEM((2, fields, members, TILE), f32),
            dma((6,)), dma((columns // CHUNK,)), dma((3, 2)), dma((3, 2)), dma((peers,)), dma((peers,)),
            dma((parts, peers)), dma((parts, peers)), dma((parts, peers)), dma((parts, peers)), dma((2,)), dma((2,)),
        ],
        compiler_params=pltpu.CompilerParams(collective_id=0, has_side_effects=True, vmem_limit_bytes=60 * 2**20),
    )(
        jnp.transpose(state, (1, 0, 2)), courant[None, :], angle[None, :],
        obs_index.reshape(nobs // TILE, TILE), obs_value[None, :], obs_variance[None, :], perturb,
    )
    return jnp.transpose(result, (1, 0, 2))


def solution(mesh):
    in_specs = (
        P("mem", None, "strip"),
        P("strip"),
        P("strip"),
        P("strip"),
        P("strip"),
        P("strip"),
        P(None, "strip"),
    )
    out_specs = P("mem", None, "strip")
    return jax.shard_map(local, mesh=mesh, in_specs=in_specs, out_specs=out_specs, check_vma=False)
```

```python
import functools

import jax
import jax.numpy as jnp
from jax import lax
from jax.experimental import pallas as pl
from jax.experimental.pallas import tpu as pltpu
from jax.sharding import PartitionSpec as P

STEPS_BEFORE = 4
STEPS_AFTER = 2
SQUARINGS = 12
EXACT = 4
ROUGH = 2
CHUNK = 1024
TILE = 128
MESH = pl.DeviceIdType.MESH
HIGH = lax.Precision.HIGHEST


def dot(a, b, dims=((1,), (0,))):
    return lax.dot_general(a, b, (dims, ((), ())), precision=HIGH, preferred_element_type=jnp.float32)


def dot3(a, b, dims=((1,), (0,))):
    def one(x, y):
        return lax.dot_general(x, y, (dims, ((), ())), preferred_element_type=jnp.float32)

    a_hi, b_hi = a.astype(jnp.bfloat16), b.astype(jnp.bfloat16)
    a_lo = (a - a_hi.astype(jnp.float32)).astype(jnp.bfloat16)
    b_lo = (b - b_hi.astype(jnp.float32)).astype(jnp.bfloat16)
    rows = a.shape[0]
    both = one(jnp.concatenate([a_hi, a_lo], axis=0), b_hi)
    return both[:rows] + (both[rows:] + one(a_hi, b_lo))


def dot1(a, b):
    return jnp.dot(a.astype(jnp.bfloat16), b.astype(jnp.bfloat16), preferred_element_type=jnp.float32)


def cosine_sine(angle):
    t = angle * angle
    cosine = 1.0 + t * (-1 / 2 + t * (1 / 24 + t * (-1 / 720 + t * (1 / 40320 - t * (1 / 3628800)))))
    sine = angle * (1.0 + t * (-1 / 6 + t * (1 / 120 + t * (-1 / 5040 + t * (1 / 362880)))))
    return cosine, sine


def advance(fields, coefs, steps):
    h, u, v = fields
    c, cosine, sine = coefs
    last = h.shape[-1] - 1
    half = 0.5 * c
    for _ in range(steps):
        a = u + h
        b = u - h
        da = a - pltpu.roll(a, 1, axis=1)
        db = pltpu.roll(b, last, axis=1) - b
        speed = u + half * (db - da)
        h = h - half * (da + db)
        u = cosine * speed + sine * v
        v = cosine * v - sine * speed
    return h, u, v


def kernel(
    state, courant, angle, obs_index, obs_value, obs_variance, perturb, out,
    fields_in, raw, coef, index, value, variance, noise, prior, observed, grid, mixed, analysed,
    halo_in, halo_raw, halo_out,
    load_sem, state_sem, halo_send, halo_recv, obs_send, obs_recv,
    in_send, in_recv, out_send, out_recv, edge_send, edge_recv,
):
    members, columns = state.shape[1], state.shape[2]
    peers = grid.shape[1] // members
    width = grid.shape[2]
    parts = width // TILE
    count = peers * members
    nobs = observed.shape[1]
    chunks = columns // CHUNK
    halves = members // 8
    me = lax.axis_index("mem")
    strip = lax.axis_index("strip")
    strips = lax.axis_size("strip")
    right = (strip + 1) % strips
    left = (strip + strips - 1) % strips
    first, last = pl.ds(0, TILE), pl.ds(columns - TILE, TILE)
    own = pl.ds(pl.multiple_of(me * members, members), members)

    barrier = pltpu.get_barrier_semaphore()

    def greet(r, carry):
        pl.semaphore_signal(barrier, inc=1, device_id={"mem": (me + r) % peers}, device_id_type=MESH)
        return carry

    lax.fori_loop(1, peers, greet, 0)
    for other in (left, right):
        pl.semaphore_signal(barrier, inc=1, device_id={"strip": other}, device_id_type=MESH)

    pairs = [
        (angle, raw.at[0]), (courant, raw.at[1]), (obs_index, index), (obs_value, value),
        (obs_variance, variance), (perturb, noise),
    ]
    loads = [pltpu.make_async_copy(a, b, load_sem.at[n]) for n, (a, b) in enumerate(pairs)]

    def state_load(k):
        at = pl.ds(k * CHUNK, CHUNK)
        to = pl.ds(TILE + k * CHUNK, CHUNK)
        return pltpu.make_async_copy(state.at[:, :, at], fields_in.at[:, :, to], state_sem.at[k])

    for load in loads[:2]:
        load.start()
    for k in range(chunks):
        state_load(k).start()
    for load in loads[2:]:
        load.start()

    pl.semaphore_wait(barrier, peers + 1)

    def to_neighbours(source, target, send, recv):
        return [
            pltpu.make_async_remote_copy(
                source.at[..., at], target.at[side], send.at[side], recv.at[side],
                device_id={"strip": other}, device_id_type=MESH,
            )
            for side, (at, other) in enumerate([(last, right), (first, left)])
        ]

    halos = (
        to_neighbours(state, halo_in, halo_send.at[0], halo_recv.at[0])
        + to_neighbours(angle, halo_raw.at[0], halo_send.at[1], halo_recv.at[1])
        + to_neighbours(courant, halo_raw.at[1], halo_send.at[2], halo_recv.at[2])
    )
    for copy in halos:
        copy.start()

    for load in loads[:2]:
        load.wait()

    def factors_of(turn, speed):
        shape = (8, turn.shape[-1])
        cosine, sine = cosine_sine(jnp.broadcast_to(turn, shape))
        return jnp.broadcast_to(speed, shape), cosine, sine

    def coefficients(k, carry):
        at = pl.ds(pl.multiple_of(k * CHUNK, CHUNK), CHUNK)
        to = pl.ds(pl.multiple_of(TILE + k * CHUNK, TILE), CHUNK)
        for f, factor in enumerate(factors_of(raw[0, :, at], raw[1, :, at])):
            coef[f, :, to] = factor
        return carry

    lax.fori_loop(0, chunks, coefficients, 0)

    def sweep(source, target, steps, k):
        window = pl.ds(pl.multiple_of(k * CHUNK, TILE), CHUNK + 2 * TILE)
        to = pl.ds(pl.multiple_of(k * CHUNK, CHUNK), CHUNK)
        factors = [coef[f, :, window] for f in range(3)]
        for half in range(halves):
            rows = pl.ds(half * 8, 8)
            news = advance([source[f, rows, window] for f in range(3)], factors, steps)
            for f in range(3):
                target[f, rows, to] = news[f][:, TILE : TILE + CHUNK]

    def sweep_ends(source, halo, target, steps, outer):
        two = [pl.ds(columns - TILE, 2 * TILE), pl.ds(TILE, 2 * TILE)]
        for side in range(2):
            inner = two[1 - side]

            def joined(edge, inside, side=side):
                return jnp.concatenate([edge, inside] if side == 0 else [inside, edge], axis=1)

            factors = [joined(outer[side][f], coef[f, :, inner]) for f in range(3)]
            for half in range(halves):
                rows = pl.ds(half * 8, 8)
                window = [joined(halo[side, f, rows, :], source[f, rows, inner]) for f in range(3)]
                news = advance(window, factors, steps)
                for f in range(3):
                    target[f, rows, (first, last)[side]] = news[f][:, TILE : 2 * TILE]

    for k in range(chunks):
        state_load(k).wait()

    def part_of(peer, q):
        return q + (peer // (peers - 1)) * (parts - 1 - 2 * q)

    def in_copy(q, r):
        peer = (me + r) % peers
        t = part_of(peer, q)
        return pltpu.make_async_remote_copy(
            prior.at[:, :, pl.ds(pl.multiple_of(peer * width + t * TILE, TILE), TILE)],
            grid.at[:, own, pl.ds(pl.multiple_of(t * TILE, TILE), TILE)],
            in_send.at[q, r], in_recv.at[q, r], device_id={"mem": peer}, device_id_type=MESH,
        )

    def each(make, action):
        def body(r, carry):
            action(make(r))
            return carry

        lax.fori_loop(1, peers, body, 0)

    for load in loads[2:]:
        load.wait()
    groups = nobs // TILE
    tiles = [jnp.broadcast_to(index[g : g + 1, :] // TILE, (8, TILE)) for g in range(groups)]
    lanes = [jnp.broadcast_to(index[g : g + 1, :] % TILE, (8, TILE)) for g in range(groups)]

    def pick(t, found):
        at = pl.ds(pl.multiple_of(t * TILE, TILE), TILE)
        news = []
        for half in range(halves):
            heights = prior[0, pl.ds(half * 8, 8), at]
            for g in range(groups):
                picked = jnp.take_along_axis(heights, lanes[g], axis=1)
                news.append(jnp.where(tiles[g] == t, picked, found[half * groups + g]))
        return tuple(news)

    blocks = CHUNK // width

    def step_and_send(i, found):
        k = (me // blocks + 1 + i) % chunks
        sweep(fields_in, prior, STEPS_BEFORE, k)
        for j in range(CHUNK // TILE):
            found = pick(k * (CHUNK // TILE) + j, found)
        for j in range(blocks):
            peer = k * blocks + j

            @pl.when(peer != me)
            def _(peer=peer):
                in_copy(1, (peer + peers - me) % peers).start()

        return found

    found = (jnp.zeros((8, TILE), jnp.float32),) * (groups * halves)
    found = lax.fori_loop(0, chunks, step_and_send, found)

    for copy in halos:
        copy.wait()
    outer = [factors_of(halo_raw[0, side], halo_raw[1, side]) for side in range(2)]
    sweep_ends(fields_in, halo_in, prior, STEPS_BEFORE, outer)
    found = pick(0, found)
    found = pick(columns // TILE - 1, found)
    for half in range(halves):
        for g in range(groups):
            rows = pl.ds(pl.multiple_of(me * members + half * 8, 8), 8)
            observed[rows, pl.ds(g * TILE, TILE)] = found[half * groups + g]

    chips = peers // 2
    sibling = me + 1 - 2 * (me % 2)

    def obs_copy(r):
        return pltpu.make_async_remote_copy(
            observed.at[own, :], observed.at[own, :], obs_send.at[r], obs_recv.at[r],
            device_id={"mem": (me + 2 * r) % peers}, device_id_type=MESH,
        )

    def obs_share(r):
        rows = pl.ds(pl.multiple_of((me + peers - 2 * r) % peers * members, members), members)
        return pltpu.make_async_remote_copy(
            observed.at[rows, :], observed.at[rows, :], obs_send.at[chips + r], obs_recv.at[chips + r],
            device_id={"mem": sibling}, device_id_type=MESH,
        )

    for r in range(1, chips):
        obs_copy(r).start()
    obs_share(0).start()
    for q in (0, 2, 3):
        each(functools.partial(in_copy, q), lambda copy: copy.start())
    grid[:, own, :] = prior[:, :, pl.ds(pl.multiple_of(me * width, width), width)]
    for r in range(1, chips):
        obs_copy(r).wait_recv()
        obs_share(r).start()
    for r in range(chips):
        obs_share(r).wait()
    for r in range(1, chips):
        obs_copy(r).wait_send()

    predicted = observed[...]
    spread = predicted - jnp.sum(predicted, axis=0, keepdims=True) * (1.0 / count)
    innovation = value[...] + noise[...] - predicted
    scaled = spread * (1.0 / variance[...])
    rows_id = lax.broadcasted_iota(jnp.int32, (count, count), 0)
    cols_id = lax.broadcasted_iota(jnp.int32, (count, count), 1)
    unit = jnp.where(rows_id == cols_id, 1.0, 0.0).astype(jnp.float32)
    low = float(count - 1)
    inner = dot(scaled, spread, ((1,), (1,))) + low * unit
    update = dot(innovation, scaled, ((1,), (1,)))
    widest = jnp.max(jnp.sum(jnp.abs(inner), axis=0, keepdims=True), axis=1, keepdims=True)
    total = jnp.sum(jnp.sum(inner * unit, axis=0, keepdims=True), axis=1, keepdims=True)
    high = jnp.minimum(widest, total)
    rate = 2.0 / (high + low)
    gap = 2.0 * low / (high + low)
    remainder = unit - rate * inner
    inverse = rate * unit
    for n in range(SQUARINGS):
        multiply = dot if n < EXACT else dot3 if n < SQUARINGS - ROUGH else dot1
        shrink = gap * (2.0 - gap)
        scale = 2.0 / (1.0 + shrink)
        gap = scale * shrink
        if n == 0:
            inverse = (scale * rate) * (unit + remainder)
            square = multiply(remainder, remainder)
        else:
            both = multiply(jnp.concatenate([remainder, inverse], axis=0), remainder)
            square, inverse = both[:count], scale * (inverse + both[count:])
        remainder = scale * square + (1.0 - scale) * unit
    inverse = inverse + dot1(inverse, remainder)
    first_try = dot(update, inverse)
    update = first_try + dot3(update - dot(first_try, inner), inverse)

    def out_copy(q, r):
        peer = (me + r) % peers
        t = part_of(me, q)
        return pltpu.make_async_remote_copy(
            mixed.at[:, pl.ds(pl.multiple_of(peer * members, members), members), pl.ds(pl.multiple_of(t * TILE, TILE), TILE)],
            analysed.at[:, :, pl.ds(pl.multiple_of(TILE + me * width + t * TILE, TILE), TILE)],
            out_send.at[q, r], out_recv.at[q, r], device_id={"mem": peer}, device_id_type=MESH,
        )

    for q in range(parts):
        each(functools.partial(in_copy, q), lambda copy: copy.wait())
        at = pl.ds(pl.multiple_of(part_of(me, q) * TILE, TILE), TILE)
        block = jnp.concatenate([grid[f, :, at] for f in range(3)], axis=1)
        block = block + dot3(update, block)
        for f in range(3):
            mixed[f, :, at] = block[:, f * TILE : (f + 1) * TILE]
        each(functools.partial(out_copy, q), lambda copy: copy.start())
    analysed[:, :, pl.ds(pl.multiple_of(TILE + me * width, TILE), width)] = mixed[:, own, :]
    each(functools.partial(out_copy, 0), lambda copy: copy.wait())
    edges = to_neighbours(analysed.at[:, :, pl.ds(TILE, columns)], halo_out, edge_send, edge_recv)
    for copy in edges:
        copy.start()
    for q in range(1, parts):
        each(functools.partial(out_copy, q), lambda copy: copy.wait())

    def last_steps(k, carry):
        sweep(analysed, out, STEPS_AFTER, k)
        return carry

    lax.fori_loop(0, chunks, last_steps, 0)
    for copy in edges:
        copy.wait()
    sweep_ends(analysed, halo_out, out, STEPS_AFTER, outer)


def local(state, courant, angle, obs_index, obs_value, obs_variance, perturb):
    members, fields, columns = state.shape
    nobs = obs_index.shape[0]
    peers = lax.axis_size("mem")
    count, width = peers * members, columns // peers
    parts, wide = width // TILE, columns + 2 * TILE
    f32 = jnp.float32
    dma = pltpu.SemaphoreType.DMA
    result = pl.pallas_call(
        kernel,
        out_shape=pltpu.VMEM((fields, members, columns), f32),
        in_specs=[pl.BlockSpec(memory_space=pltpu.HBM)] * 7,
        out_specs=pl.BlockSpec(memory_space=pltpu.VMEM),
        scratch_shapes=[
            pltpu.VMEM((fields, members, wide), f32),
            pltpu.VMEM((2, 1, columns), f32),
            pltpu.VMEM((3, 8, wide), f32),
            pltpu.VMEM((nobs // TILE, TILE), jnp.int32),
            pltpu.VMEM((1, nobs), f32),
            pltpu.VMEM((1, nobs), f32),
            pltpu.VMEM((count, nobs), f32),
            pltpu.VMEM((fields, members, columns), f32),
            pltpu.VMEM((count, nobs), f32),
            pltpu.VMEM((fields, count, width), f32),
            pltpu.VMEM((fields, count, width), f32),
            pltpu.VMEM((fields, members, wide), f32),
            pltpu.VMEM((2, fields, members, TILE), f32),
            pltpu.VMEM((2, 2, 1, TILE), f32),
            pltpu.VMEM((2, fields, members, TILE), f32),
            dma((6,)), dma((columns // CHUNK,)), dma((3, 2)), dma((3, 2)), dma((peers,)), dma((peers,)),
            dma((parts, peers)), dma((parts, peers)), dma((parts, peers)), dma((parts, peers)), dma((2,)), dma((2,)),
        ],
        compiler_params=pltpu.CompilerParams(collective_id=0, has_side_effects=True, vmem_limit_bytes=60 * 2**20),
    )(
        jnp.transpose(state, (1, 0, 2)), courant[None, :], angle[None, :],
        obs_index.reshape(nobs // TILE, TILE), obs_value[None, :], obs_variance[None, :], perturb,
    )
    return jnp.transpose(result, (1, 0, 2))


def solution(mesh):
    in_specs = (
        P("mem", None, "strip"),
        P("strip"),
        P("strip"),
        P("strip"),
        P("strip"),
        P("strip"),
        P(None, "strip"),
    )
    out_specs = P("mem", None, "strip")
    return jax.shard_map(local, mesh=mesh, in_specs=in_specs, out_specs=out_specs, check_vma=False)
```
